512 devices in a mesh: row: 32 (over y_hi, z), col: 16 (over x, y_lo, core).
Axes of the slice: x: 4, y: 8 (y_hi: 4, y_lo: 2; y = y_hi * 2 + y_lo), z: 8, core: 2. Of those that a mesh axis runs over, the one named last changes fastest.
Arguments:
- features: bfloat16 [65536, 128], P(('col', 'row')), may hold values from -6 to 6
- adj_blocks: bfloat16 [32, 16, 128, 128, 128], P('row', 'col'), may hold values from -0.046875 to 0.046875
- block_rows: int32 [32, 16, 128], P('row', 'col'), may hold values from 0 to 15, as said below
- block_cols: int32 [32, 16, 128], P('row', 'col'), may hold values from 0 to 31, as said below
- block_counts: int32 [32, 16], P('row', 'col'), may hold values from 32 to 128, as said below
- weight: bfloat16 [128, 128], replicated, may hold values from -0.5 to 0.5
- pre_act: bfloat16 [65536, 128], P(('row', 'col')), may hold values from -6 to 6
- upstream: bfloat16 [65536, 128], P(('row', 'col')), may hold values from -6 to 6
Outputs:
- aggregated: bfloat16 [65536, 128], P(('row', 'col'))
- weight_grad: float32 [128, 128], replicated
- agg_grad: bfloat16 [65536, 128], P(('row', 'col'))
The draws below stay inside these ranges and needn't reach their ends.
Inputs may be any that keep to these rules, and one draw needn't show every extreme that they name: On every grid cell, block_rows and block_cols together name 128 different blocks. `block_cols`: see block_rows. `block_counts`: some grid cell holds exactly 128 live blocks in every draw.
All inputs are finite; a program needn't handle non-finite values.
Results may differ from the reference program's by a relative error of at most 0.011.
Values may be sent and summed in bfloat16 or wider, within the bound.
A program may use at most 64 MiB of HBM per device.

```python
import math
import jax
import jax.numpy as jnp
from jax import lax

F = 128
BLK = 128
BLOCKS_DEV = 1
NNZB = 128
NODES = 65536
N_ROW = 32
N_COL = 16


def block_layout(key):
    cells = jax.random.split(key, N_ROW * N_COL)
    total = BLOCKS_DEV * N_COL * BLOCKS_DEV * N_ROW
    picks = jax.vmap(lambda k: jax.random.permutation(k, total)[:NNZB])(cells)
    return picks.reshape(N_ROW, N_COL, NNZB).astype(jnp.int32)


def draw_block_rows(key, part):
    picks = block_layout(key)
    return (picks // (BLOCKS_DEV * N_ROW)).astype(jnp.int32)


def draw_block_cols(key, part):
    picks = block_layout(key)
    return (picks % (BLOCKS_DEV * N_ROW)).astype(jnp.int32)


def draw_block_counts(key, part):
    key = jax.random.fold_in(key, 7)
    first, second = jax.random.split(key)
    counts = jax.random.randint(first, (N_ROW * N_COL,), max(NNZB // 4, 1), NNZB + 1)
    fullest = jax.random.randint(second, (), 0, N_ROW * N_COL)
    counts = jnp.where(jnp.arange(N_ROW * N_COL) == fullest, NNZB, counts)
    return counts.reshape(N_ROW, N_COL).astype(jnp.int32)


def block_scale(own_key, extent, cuts, least, high):
    factor_of = 1.0
    for dim, parts in cuts:
        heights = jax.random.uniform(jax.random.fold_in(jax.random.fold_in(own_key, 6), dim), (parts,), jnp.float32, least / len(cuts), high / len(cuts))
        factor_of = factor_of * jnp.repeat(jnp.exp(heights), extent[dim] // parts).reshape((-1,) + (1,) * (len(extent) - 1 - dim))
    return factor_of


def centred(key, extent, deviation, most, shards=(), kind=jnp.bfloat16):
    drawn = deviation * jax.random.normal(key, extent, jnp.float32)
    if shards:
        drawn = drawn * block_scale(key, extent, shards, -0.22, 0.18)
    return jnp.clip(drawn, -most, most).astype(kind)


def setup_inputs(seed: int = 0) -> dict:
    key_of = jax.random.split(jax.random.key(seed), 9)
    return {
        "features": centred(key_of[0], (NODES, F), 1.0, 6.0, ((0, 512),)),
        "adj_blocks": centred(key_of[1], (N_ROW, N_COL, NNZB, BLK, BLK), (BLK * NNZB // BLOCKS_DEV) ** -0.5, 0.046875, ((0, 32), (1, 16))),
        "block_rows": draw_block_rows(jax.random.fold_in(key_of[8], 71), 0),
        "block_cols": draw_block_cols(jax.random.fold_in(key_of[8], 71), 0),
        "block_counts": draw_block_counts(jax.random.fold_in(key_of[8], 71), 0),
        "weight": centred(key_of[5], (F, F), F ** -0.5, 0.5),
        "pre_act": centred(key_of[6], (NODES, F), 1.0, 6.0, ((0, 512),)),
        "upstream": centred(key_of[7], (NODES, F), 1.0, 6.0, ((0, 512),)),
    }


def reference(features, adj_blocks, block_rows, block_cols, block_counts, weight, pre_act, upstream):
    width = features.shape[1]
    row_blocks = BLOCKS_DEV * N_COL
    panels = features.reshape(N_COL, BLOCKS_DEV * N_ROW, BLK, width)

    def one_row(r):

        def one_cell(c):
            tiles = panels[c][block_cols[r, c]].astype(jnp.float32)
            prods = jnp.einsum('bij,bjf->bif', adj_blocks[r, c].astype(jnp.float32), tiles)
            live = jnp.arange(NNZB) < block_counts[r, c]
            prods = jnp.where(live[:, None, None], prods, jnp.float32(0.0))
            return jax.ops.segment_sum(prods, block_rows[r, c], num_segments=row_blocks)
        return lax.optimization_barrier(jnp.sum(lax.map(one_cell, jnp.arange(N_COL)), axis=0))
    summed = lax.map(one_row, jnp.arange(N_ROW))
    aggregated = summed.reshape(NODES, width).astype(jnp.bfloat16)
    grad_pre = jnp.where(pre_act > 0, upstream, jnp.zeros_like(upstream))
    agg_grad = jnp.dot(grad_pre, weight.T, preferred_element_type=jnp.float32).astype(jnp.bfloat16)
    weight_grad = jnp.dot(aggregated.T, grad_pre, preferred_element_type=jnp.float32)
    weight_grad = weight_grad * jnp.float32(1.0 / math.sqrt(NODES))
    return (aggregated, weight_grad, agg_grad)
```

```python
import functools
import math

import jax
import jax.numpy as jnp
from jax import lax
from jax.experimental import pallas as pl
from jax.experimental.pallas import tpu as pltpu
from jax.sharding import PartitionSpec as P

MESH = pl.DeviceIdType.MESH
NY = 4
NZ = 8
NR = NY * NZ
NC = 16
BLK = 128
ROWS = NC * BLK
GROUP = 4
SLICE = BLK // NC


def kernel(
    scale,
    table,
    feat,
    adj,
    weight,
    pre_act,
    upstream,
    agg_out,
    wg_out,
    grad_out,
    a_v,
    x_v,
    acc,
    part,
    parts_in,
    w_loc,
    w_in1,
    w_mid,
    w_in2,
    w_fin,
    a_sem,
    y_send,
    y_recv,
    z_send,
    z_recv,
    r_sem,
    w_sem,
):
    row = lax.axis_index("row")
    col = lax.axis_index("col")
    y = row // NZ
    z = row % NZ

    barrier = pltpu.get_barrier_semaphore()

    def hello_row(k, _):
        pl.semaphore_signal(
            barrier, inc=1, device_id=((row + k) % NR, col), device_id_type=MESH
        )
        return 0

    def hello_col(k, _):
        pl.semaphore_signal(
            barrier, inc=1, device_id=(row, (col + k) % NC), device_id_type=MESH
        )
        return 0

    lax.fori_loop(1, NR, hello_row, 0)
    lax.fori_loop(1, NC, hello_col, 0)

    load_a = pltpu.make_async_copy(adj, a_v.at[pl.ds(0, adj.shape[0])], a_sem)
    load_a.start()
    x_v[row] = feat[...]
    a_v[adj.shape[0]] = jnp.zeros((BLK, BLK), jnp.bfloat16)
    acc[...] = jnp.zeros_like(acc)
    grad_pre = jnp.where(
        pre_act[...].astype(jnp.float32) > 0, upstream[...].astype(jnp.float32), 0.0
    ).astype(jnp.bfloat16)
    grad_out[...] = lax.dot_general(
        grad_pre, weight[...], (((1,), (1,)), ((), ())), preferred_element_type=jnp.float32
    ).astype(jnp.bfloat16)

    pl.semaphore_wait(barrier, NR - 1 + NC - 1)

    def block_of(j, zz):
        return ((y + j) % NY) * NZ + zz

    def y_copy(j):
        return pltpu.make_async_remote_copy(
            src_ref=x_v.at[row],
            dst_ref=x_v.at[row],
            send_sem=y_send.at[j - 1],
            recv_sem=y_recv.at[j - 1],
            device_id=(block_of(NY - j, z), col),
            device_id_type=MESH,
        )

    def z_copy(up, k, j):
        if up:
            src, dst, d = (z - (k - 1) + NZ) % NZ, (z + 1) % NZ, 0
        else:
            src, dst, d = (z + (k - 1)) % NZ, (z - 1 + NZ) % NZ, 1
        b = block_of(j, src)
        return pltpu.make_async_remote_copy(
            src_ref=x_v.at[b],
            dst_ref=x_v.at[b],
            send_sem=z_send.at[d, (k - 1) * NY + j],
            recv_sem=z_recv.at[d, (k - 1) * NY + j],
            device_id=(block_of(0, dst), col),
            device_id_type=MESH,
        )

    z_copy(True, 1, 0).start()
    z_copy(False, 1, 0).start()
    for j in range(1, NY):
        y_copy(j).start()
    for j in range(1, NY):
        y_copy(j).wait_recv()
        z_copy(True, 1, j).start()
        z_copy(False, 1, j).start()
    load_a.wait()

    def multiply(b0, b1):
        tiles = jnp.concatenate([x_v[b0], x_v[b1]], axis=0)
        for g in range(NC // GROUP):
            lhs = jnp.concatenate(
                [
                    jnp.concatenate(
                        [a_v[table[b0 * NC + r]], a_v[table[b1 * NC + r]]], axis=1
                    )
                    for r in range(g * GROUP, (g + 1) * GROUP)
                ],
                axis=0,
            )
            span = pl.ds(g * GROUP * BLK, GROUP * BLK)
            acc[span, :] += jnp.dot(lhs, tiles, preferred_element_type=jnp.float32)

    def step(s, _):
        t = s - 2
        k = t // NY + 1
        j = t % NY
        ring = (s >= 2) & (s < 14)

        @pl.when(ring)
        def _():
            z_copy(True, k, j).wait_recv()

            @pl.when((k < 3) | (j < 2))
            def _():
                z_copy(True, k + 1, j).start()

            z_copy(False, k, j).wait_recv()

            @pl.when((k < 3) | (j >= 2))
            def _():
                z_copy(False, k + 1, j).start()

        @pl.when(s == 14)
        def _():
            z_copy(True, 4, 0).wait_recv()
            z_copy(True, 4, 1).wait_recv()

        @pl.when(s == 15)
        def _():
            z_copy(False, 4, 2).wait_recv()
            z_copy(False, 4, 3).wait_recv()

        far = (z + 4) % NZ
        own = s < 2
        last0 = (s - 14) * 2
        j0 = jnp.where(own, 2 * s, jnp.where(ring, j, last0))
        j1 = jnp.where(own, 2 * s + 1, jnp.where(ring, j, last0 + 1))
        z0 = jnp.where(own, z, jnp.where(ring, (z - k + NZ) % NZ, far))
        z1 = jnp.where(own, z, jnp.where(ring, (z + k) % NZ, far))
        multiply(block_of(j0, z0), block_of(j1, z1))
        return 0

    lax.fori_loop(0, NR // 2, step, 0)

    def part_copy(k):
        to = (col + k) % NC
        return pltpu.make_async_remote_copy(
            src_ref=part.at[to],
            dst_ref=parts_in.at[NC - 1 - k],
            send_sem=r_sem.at[0],
            recv_sem=r_sem.at[1],
            device_id=(row, to),
            device_id_type=MESH,
        )

    def send_part(k, _):
        to = (col + k) % NC
        part[to] = acc[pl.ds(pl.multiple_of(to * BLK, BLK), BLK), :].astype(jnp.bfloat16)
        part_copy(k).start()
        return 0

    lax.fori_loop(1, NC, send_part, 0)
    whole = parts_in.at[pl.ds(0, NC - 1)]
    pltpu.make_async_copy(whole, whole, r_sem.at[1]).wait()
    total = acc[pl.ds(pl.multiple_of(col * BLK, BLK), BLK), :]
    for k in range(NC - 1):
        total = total + parts_in[k].astype(jnp.float32)
    aggregated = total.astype(jnp.bfloat16)
    agg_out[...] = aggregated

    term = lax.dot_general(
        aggregated, grad_pre, (((0,), (0,)), ((), ())), preferred_element_type=jnp.float32
    )
    w_loc[...] = term.reshape(NC, SLICE, BLK)

    def scatter(k, _):
        to = (col + k) % NC
        pltpu.make_async_remote_copy(
            src_ref=w_loc.at[to],
            dst_ref=w_in1.at[NC - 1 - k],
            send_sem=w_sem.at[0],
            recv_sem=w_sem.at[1],
            device_id=(row, to),
            device_id_type=MESH,
        ).start()
        return 0

    lax.fori_loop(1, NC, scatter, 0)
    some = w_in1.at[pl.ds(0, NC - 1)]
    pltpu.make_async_copy(some, some, w_sem.at[1]).wait()
    mid = w_loc[col]
    for k in range(NC - 1):
        mid = mid + w_in1[k]
    w_mid[...] = mid
    w_in2[row] = mid

    def exchange(k, _):
        pltpu.make_async_remote_copy(
            src_ref=w_mid,
            dst_ref=w_in2.at[row],
            send_sem=w_sem.at[2],
            recv_sem=w_sem.at[3],
            device_id=((row + k) % NR, col),
            device_id_type=MESH,
        ).start()
        return 0

    lax.fori_loop(1, NR, exchange, 0)
    some = w_in2.at[pl.ds(0, NR - 1)]
    pltpu.make_async_copy(some, some, w_sem.at[3]).wait()
    fin = w_in2[0]
    for k in range(1, NR):
        fin = fin + w_in2[k]
    w_fin[col] = fin * scale

    def gather(k, _):
        pltpu.make_async_remote_copy(
            src_ref=w_fin.at[col],
            dst_ref=w_fin.at[col],
            send_sem=w_sem.at[4],
            recv_sem=w_sem.at[5],
            device_id=(row, (col + k) % NC),
            device_id_type=MESH,
        ).start()
        return 0

    lax.fori_loop(1, NC, gather, 0)
    some = w_fin.at[pl.ds(0, NC - 1)]
    pltpu.make_async_copy(some, some, w_sem.at[5]).wait()
    wg_out[...] = w_fin[...].reshape(BLK, BLK)

    for j in range(1, NY):
        y_copy(j).wait_send()
    for k in range(1, 5):
        for j in range(NY):
            if k < 4 or j < 2:
                z_copy(True, k, j).wait_send()
            if k < 4 or j >= 2:
                z_copy(False, k, j).wait_send()
    pltpu.make_async_copy(whole, whole, r_sem.at[0]).wait()
    some = w_in1.at[pl.ds(0, NC - 1)]
    pltpu.make_async_copy(some, some, w_sem.at[0]).wait()
    some = w_in2.at[pl.ds(0, NR - 1)]
    pltpu.make_async_copy(some, some, w_sem.at[2]).wait()
    some = w_fin.at[pl.ds(0, NC - 1)]
    pltpu.make_async_copy(some, some, w_sem.at[4]).wait()


def per_device(
    features, adj_blocks, block_rows, block_cols, block_counts, weight, pre_act, upstream
):
    blocks = adj_blocks[0, 0]
    slots = blocks.shape[0]
    slot = jnp.arange(slots, dtype=jnp.int32)
    place = block_cols[0, 0] * NC + block_rows[0, 0]
    hit = (place[None, :] == jnp.arange(NR * NC, dtype=jnp.int32)[:, None]) & (
        slot < block_counts[0, 0]
    )[None, :]
    table = slots + jnp.sum(jnp.where(hit, slot[None, :] - slots, 0), axis=1)

    vmem = pl.BlockSpec(memory_space=pltpu.VMEM)
    bf16, f32 = jnp.bfloat16, jnp.float32
    nodes = BLK * NR * NC
    return pl.pallas_call(
        functools.partial(kernel, 1.0 / math.sqrt(nodes)),
        out_shape=(
            jax.ShapeDtypeStruct((BLK, BLK), bf16),
            jax.ShapeDtypeStruct((BLK, BLK), f32),
            jax.ShapeDtypeStruct((BLK, BLK), bf16),
        ),
        in_specs=[
            pl.BlockSpec(memory_space=pltpu.SMEM),
            vmem,
            pl.BlockSpec(memory_space=pl.ANY),
            vmem,
            vmem,
            vmem,
        ],
        out_specs=(vmem, vmem, vmem),
        scratch_shapes=[
            pltpu.VMEM((slots + 1, BLK, BLK), bf16),
            pltpu.VMEM((NR, BLK, BLK), bf16),
            pltpu.VMEM((ROWS, BLK), f32),
            pltpu.VMEM((NC, BLK, BLK), bf16),
            pltpu.VMEM((NC, BLK, BLK), bf16),
            pltpu.VMEM((NC, SLICE, BLK), f32),
            pltpu.VMEM((NC, SLICE, BLK), f32),
            pltpu.VMEM((SLICE, BLK), f32),
            pltpu.VMEM((NR, SLICE, BLK), f32),
            pltpu.VMEM((NC, SLICE, BLK), f32),
            pltpu.SemaphoreType.DMA,
            pltpu.SemaphoreType.DMA((NY - 1,)),
            pltpu.SemaphoreType.DMA((NY - 1,)),
            pltpu.SemaphoreType.DMA((2, 16)),
            pltpu.SemaphoreType.DMA((2, 16)),
            pltpu.SemaphoreType.DMA((2,)),
            pltpu.SemaphoreType.DMA((6,)),
        ],
        compiler_params=pltpu.CompilerParams(
            collective_id=0, has_side_effects=True, vmem_limit_bytes=40 * 1024 * 1024
        ),
        name="gcn",
    )(table, features, blocks, weight, pre_act, upstream)


def solution(mesh):
    placed = (
        P(("col", "row"), None),
        P("row", "col", None, None, None),
        P("row", "col", None),
        P("row", "col", None),
        P("row", "col"),
        P(),
        P(("row", "col"), None),
        P(("row", "col"), None),
    )
    return jax.shard_map(
        per_device,
        mesh=mesh,
        in_specs=placed,
        out_specs=(P(("row", "col"), None), P(), P(("row", "col"), None)),
        check_vma=False,
    )
```

```python
import functools
import math

import jax
import jax.numpy as jnp
from jax import lax
from jax.experimental import pallas as pl
from jax.experimental.pallas import tpu as pltpu
from jax.sharding import PartitionSpec as P

MESH = pl.DeviceIdType.MESH
NY = 4
NZ = 8
NR = NY * NZ
NX = 4
NC = 16
NQ = NX * 2
BLK = 128
ROWS = NC * BLK
GROUP = 4
SLICE = BLK // NQ
NEAR = ((), (1, 7, 2, 6), (1, 7, 2, 6, 3), (1, 7, 2, 6))
FAR = (3, 5, 4)


def wrap(t, n):
    return jnp.where(t >= n, t - n, t)


def kernel(
    scale,
    table_h,
    feat_h,
    adj_h,
    weight_h,
    pre_h,
    up_h,
    agg_out,
    wg_out,
    grad_out,
    table,
    w_v,
    pre_v,
    up_v,
    a_v,
    x_v,
    g_v,
    acc,
    part,
    parts_in,
    w_loc,
    w_in1,
    w_my,
    w_iny,
    w_mz,
    w_inz,
    w_fin,
    in_sem,
    x_send,
    x_recv,
    g_sem,
    r_sem,
    w_sem,
):
    row = lax.axis_index("row")
    col = lax.axis_index("col")
    y = row // NZ
    z = row - y * NZ
    x = col // 4
    y_lo = (col // 2) % 2
    core = col % 2
    slots = adj_h.shape[0]

    def at(j, d):
        return wrap(y + j, NY) * NZ + wrap(z + d, NZ)

    def over(i, m, c):
        return wrap(x + i, NX) * 4 + wrap(y_lo + m, 2) * 2 + wrap(core + c, 2)

    z_peers = [(at(0, d), col) for d in range(1, NZ)]
    y_peers = [
        (at(j, 0), over(0, m, 0)) for j in range(NY) for m in range(2) if j or m
    ]
    col_peers = [
        (row, over(i, m, c))
        for i in range(NX)
        for m in range(2)
        for c in range(2)
        if i or m or c
    ]
    far_y = [(at(j, 0), over(0, 1, 0)) for j in range(1, NY)]
    near_y = [(at(j, 0), col) for j in range(1, NY)]

    barrier = pltpu.get_barrier_semaphore()
    hello = z_peers + near_y + far_y + col_peers
    for peer in hello:
        pl.semaphore_signal(barrier, inc=1, device_id=peer, device_id_type=MESH)

    loads = [
        pltpu.make_async_copy(feat_h, x_v.at[row], in_sem.at[0]),
        pltpu.make_async_copy(pre_h, pre_v, in_sem.at[1]),
        pltpu.make_async_copy(up_h, up_v, in_sem.at[2]),
        pltpu.make_async_copy(weight_h, w_v, in_sem.at[3]),
        pltpu.make_async_copy(table_h, table, in_sem.at[4]),
        pltpu.make_async_copy(adj_h, a_v.at[pl.ds(0, slots)], in_sem.at[5]),
    ]
    for load in loads:
        load.start()
    a_v[slots] = jnp.zeros((BLK, BLK), jnp.bfloat16)
    acc[...] = jnp.zeros_like(acc)
    for load in loads[:4]:
        load.wait()
    grad_pre = jnp.where(
        pre_v[...].astype(jnp.float32) > 0, up_v[...].astype(jnp.float32), 0.0
    )
    pair = x * 2 + y_lo
    g_v[core, pair] = grad_pre.T.astype(jnp.bfloat16)
    grad_out[...] = lax.dot_general(
        grad_pre.astype(jnp.bfloat16),
        w_v[...],
        (((1,), (1,)), ((), ())),
        preferred_element_type=jnp.float32,
    ).astype(jnp.bfloat16)

    pl.semaphore_wait(barrier, len(hello))

    def forward(b, to, j, d):
        pltpu.make_async_remote_copy(
            src_ref=x_v.at[b],
            dst_ref=x_v.at[b],
            send_sem=x_send,
            recv_sem=x_recv.at[j * NZ + d],
            device_id=(to, col),
            device_id_type=MESH,
        ).start()

    def arrived(j, d):
        b = at(j, d)
        pltpu.make_async_copy(x_v.at[b], x_v.at[b], x_recv.at[j * NZ + d]).wait()

    for j in (2, 1, 3):
        forward(row, at(NY - j, 0), j, 0)
    for d in (4, 3, 5, 2, 6, 1, 7):
        forward(row, at(0, NZ - d), 0, d)
    for i in range(NX):
        for m in range(2):
            if i or m:
                pltpu.make_async_remote_copy(
                    src_ref=g_v.at[core, pair],
                    dst_ref=g_v.at[core, pair],
                    send_sem=g_sem.at[0],
                    recv_sem=g_sem.at[1],
                    device_id=(row, over(i, m, 0)),
                    device_id_type=MESH,
                ).start()

    for j in (1, 3):
        arrived(j, 0)
        for d in NEAR[j]:
            forward(at(j, 0), at(0, NZ - d), j, d)
    for d in FAR[:2]:
        arrived(0, d)
        for j in (1, 3, 2):
            if d not in NEAR[j]:
                forward(at(0, d), at(NY - j, 0), j, d)
    arrived(2, 0)
    for d in NEAR[2]:
        forward(at(2, 0), at(0, NZ - d), 2, d)
    arrived(0, 4)
    for j in (1, 3, 2):
        forward(at(0, 4), at(NY - j, 0), j, 4)
    for load in loads[4:]:
        load.wait()

    def multiply(b0, b1):
        tiles = jnp.concatenate([x_v[b0], x_v[b1]], axis=0)
        for g in range(NC // GROUP):
            lhs = jnp.concatenate(
                [
                    jnp.concatenate(
                        [a_v[table[b0 * NC + r]], a_v[table[b1 * NC + r]]], axis=1
                    )
                    for r in range(g * GROUP, (g + 1) * GROUP)
                ],
                axis=0,
            )
            span = pl.ds(g * GROUP * BLK, GROUP * BLK)
            acc[span, :] += jnp.dot(lhs, tiles, preferred_element_type=jnp.float32)

    all_g = g_v.at[0, pl.ds(0, NQ - 1)]
    sibling = pltpu.make_async_remote_copy(
        src_ref=g_v.at[core],
        dst_ref=g_v.at[core],
        send_sem=g_sem.at[2],
        recv_sem=g_sem.at[3],
        device_id=(row, over(0, 0, 1)),
        device_id_type=MESH,
    )

    def step(s, _):
        o = s // 2
        p = s - 2 * o
        d = jnp.where(o % 2 == 1, (o + 1) // 2, (NZ - o // 2) % NZ)

        @pl.when((o > 0) & (p == 0))
        def _():
            @pl.when((d < 3) | (d > 5))
            def _():
                arrived(0, d)

            arrived(1, d)

        @pl.when((o > 0) & (p == 1))
        def _():
            arrived(2, d)
            arrived(3, d)

        @pl.when(s == 4)
        def _():
            pltpu.make_async_copy(all_g, all_g, g_sem.at[1]).wait()
            sibling.start()

        multiply(at(2 * p, d), at(2 * p + 1, d))
        return 0

    lax.fori_loop(0, NR // 2, step, 0)

    sibling.wait_recv()
    part[...] = acc[...].reshape(NC, BLK, BLK).astype(jnp.bfloat16)
    term = jnp.zeros((BLK, BLK), jnp.float32)
    for i in range(NQ):
        term = term + jnp.dot(
            jnp.concatenate([g_v[0, i], g_v[1, i]], axis=1),
            part[2 * i : 2 * i + 2].reshape(2 * BLK, BLK),
            preferred_element_type=jnp.float32,
        )
    w_loc[...] = term.reshape(NQ, SLICE, BLK)

    q = x * 2 + core
    y_at = y * 2 + y_lo
    q_peers = [(i, c) for i in range(NX) for c in range(2) if i or c]

    def slot_of(i, c):
        return wrap(x + i, NX) * 2 + wrap(core + c, 2)

    def send(src, dst, k, peer):
        pltpu.make_async_remote_copy(
            src_ref=src,
            dst_ref=dst,
            send_sem=w_sem.at[2 * k],
            recv_sem=w_sem.at[2 * k + 1],
            device_id=peer,
            device_id_type=MESH,
        ).start()

    def total(buf):
        t = buf[0]
        for k in range(1, buf.shape[0]):
            t = t + buf[k]
        return t

    def seven(buf, sem):
        some = buf.at[pl.ds(0, 7)]
        pltpu.make_async_copy(some, some, sem).wait()

    for i, c in q_peers:
        send(w_loc.at[slot_of(i, c)], w_in1.at[q], 0, (row, over(i, 0, c)))
    w_in1[q] = w_loc[q]
    seven(w_in1, w_sem.at[1])
    mid = total(w_in1)
    w_my[...] = mid
    for peer in y_peers:
        send(w_my, w_iny.at[y_at], 1, peer)
    w_iny[y_at] = mid

    for k in range(1, NC):
        to = wrap(col + k, NC)
        pltpu.make_async_remote_copy(
            src_ref=part.at[to],
            dst_ref=parts_in.at[NC - 1 - k],
            send_sem=r_sem.at[0],
            recv_sem=r_sem.at[1],
            device_id=(row, to),
            device_id_type=MESH,
        ).start()

    seven(w_iny, w_sem.at[3])
    mid = total(w_iny)
    w_mz[...] = mid
    for peer in z_peers:
        send(w_mz, w_inz.at[z], 2, peer)
    w_inz[z] = mid

    whole = parts_in.at[pl.ds(0, NC - 1)]
    pltpu.make_async_copy(whole, whole, r_sem.at[1]).wait()
    mine = acc[pl.ds(pl.multiple_of(col * BLK, BLK), BLK), :]
    for k in range(NC - 1):
        mine = mine + parts_in[k].astype(jnp.float32)
    agg_out[...] = mine.astype(jnp.bfloat16)

    seven(w_inz, w_sem.at[5])
    w_fin[q] = total(w_inz) * scale
    for i, c in q_peers:
        send(w_fin.at[q], w_fin.at[q], 3, (row, over(i, 0, c)))
    seven(w_fin, w_sem.at[7])
    wg_out[...] = w_fin[...].reshape(BLK, BLK).T

    most = x_v.at[pl.ds(0, NR - 1)]
    pltpu.make_async_copy(most, most, x_send).wait()
    pltpu.make_async_copy(all_g, all_g, g_sem.at[0]).wait()
    sibling.wait_send()
    pltpu.make_async_copy(whole, whole, r_sem.at[0]).wait()
    for k, buf in enumerate((w_in1, w_iny, w_inz, w_fin)):
        seven(buf, w_sem.at[2 * k])


def per_device(
    features, adj_blocks, block_rows, block_cols, block_counts, weight, pre_act, upstream
):
    blocks = adj_blocks[0, 0]
    slots = blocks.shape[0]
    slot = jnp.arange(slots, dtype=jnp.int32)
    place = block_cols[0, 0] * NC + block_rows[0, 0]
    hit = (place[None, :] == jnp.arange(NR * NC, dtype=jnp.int32)[:, None]) & (
        slot < block_counts[0, 0]
    )[None, :]
    table = slots + jnp.sum(jnp.where(hit, slot[None, :] - slots, 0), axis=1)

    vmem = pl.BlockSpec(memory_space=pltpu.VMEM)
    hbm = pl.BlockSpec(memory_space=pltpu.HBM)
    bf16, f32 = jnp.bfloat16, jnp.float32
    nodes = BLK * NR * NC
    wide = (8, SLICE, BLK)
    dma = pltpu.SemaphoreType.DMA
    return pl.pallas_call(
        functools.partial(kernel, 1.0 / math.sqrt(nodes)),
        out_shape=(
            jax.ShapeDtypeStruct((BLK, BLK), bf16),
            jax.ShapeDtypeStruct((BLK, BLK), f32),
            jax.ShapeDtypeStruct((BLK, BLK), bf16),
        ),
        in_specs=[hbm] * 6,
        out_specs=(vmem, vmem, vmem),
        scratch_shapes=[
            pltpu.SMEM((NR * NC,), jnp.int32),
            pltpu.VMEM((BLK, BLK), bf16),
            pltpu.VMEM((BLK, BLK), bf16),
            pltpu.VMEM((BLK, BLK), bf16),
            pltpu.VMEM((slots + 1, BLK, BLK), bf16),
            pltpu.VMEM((NR, BLK, BLK), bf16),
            pltpu.VMEM((2, NQ, BLK, BLK), bf16),
            pltpu.VMEM((ROWS, BLK), f32),
            pltpu.VMEM((NC, BLK, BLK), bf16),
            pltpu.VMEM((NC, BLK, BLK), bf16),
            pltpu.VMEM(wide, f32),
            pltpu.VMEM(wide, f32),
            pltpu.VMEM((SLICE, BLK), f32),
            pltpu.VMEM(wide, f32),
            pltpu.VMEM((SLICE, BLK), f32),
            pltpu.VMEM(wide, f32),
            pltpu.VMEM(wide, f32),
            dma((6,)),
            dma,
            dma((NR,)),
            dma((4,)),
            dma((2,)),
            dma((8,)),
        ],
        compiler_params=pltpu.CompilerParams(
            collective_id=0, has_side_effects=True, vmem_limit_bytes=63 * 1024 * 1024
        ),
        name="gcn",
    )(table, features, blocks, weight, pre_act, upstream)


def solution(mesh):
    placed = (
        P(("col", "row"), None),
        P("row", "col", None, None, None),
        P("row", "col", None),
        P("row", "col", None),
        P("row", "col"),
        P(),
        P(("row", "col"), None),
        P(("row", "col"), None),
    )
    return jax.shard_map(
        per_device,
        mesh=mesh,
        in_specs=placed,
        out_specs=(P(("row", "col"), None), P(), P(("row", "col"), None)),
        check_vma=False,
    )
```

```python
import functools
import math

import jax
import jax.numpy as jnp
from jax import lax
from jax.experimental import pallas as pl
from jax.experimental.pallas import tpu as pltpu
from jax.sharding import PartitionSpec as P

MESH = pl.DeviceIdType.MESH
NY = 4
NZ = 8
NR = NY * NZ
NX = 4
NC = 16
NQ = NX * 2
BLK = 128
ROWS = NC * BLK
VMEM_BYTES = 63 * 1024 * 1024
GROUP = 2
SLICE = BLK // NQ
NEAR = ((), (1, 7, 2, 6), (1, 7, 2, 6, 3), (1, 7, 2, 6))
FAR = (3, 5, 4)
Z_ORDER = (4, 3, 5, 2, 6, 1, 7)


def wrap(t, n):
    return jnp.where(t >= n, t - n, t)


def kernel(
    scale,
    rows_h,
    cols_h,
    count_h,
    feat_h,
    adj_h,
    weight_h,
    pre_h,
    up_h,
    agg_out,
    wg_out,
    grad_out,
    table,
    table_v,
    rows_v,
    cols_v,
    count,
    w_v,
    pre_v,
    up_v,
    a_v,
    x_v,
    g_v,
    acc,
    part,
    parts_in,
    w_loc,
    w_in1,
    w_my,
    w_iny,
    w_mz,
    w_inz,
    w_fin,
    in_sem,
    x_send,
    x_recv,
    g_sem,
    r_sem,
    w_sem,
):
    row = lax.axis_index("row")
    col = lax.axis_index("col")
    y = row // NZ
    z = row - y * NZ
    x = col // 4
    y_lo = (col // 2) % 2
    core = col % 2
    slots = adj_h.shape[0]

    def at(j, d):
        return wrap(y + j, NY) * NZ + wrap(z + d, NZ)

    def over(i, m, c):
        return wrap(x + i, NX) * 4 + wrap(y_lo + m, 2) * 2 + wrap(core + c, 2)

    z_peers = [(at(0, d), col) for d in Z_ORDER]
    y_peers = [
        (at(j, 0), over(0, m, 0)) for j in (2, 1, 3, 0) for m in range(2) if j or m
    ]
    col_peers = [
        (row, over(i, m, c))
        for i in (2, 1, 3, 0)
        for m in range(2)
        for c in range(2)
        if i or m or c
    ]
    far_y = [(at(j, 0), over(0, 1, 0)) for j in (2, 1, 3)]
    near_y = [(at(j, 0), col) for j in (2, 1, 3)]

    barrier = pltpu.get_barrier_semaphore()
    hello = z_peers + near_y + far_y + col_peers
    for peer in hello:
        pl.semaphore_signal(barrier, inc=1, device_id=peer, device_id_type=MESH)

    loads = [
        pltpu.make_async_copy(feat_h, x_v.at[row], in_sem.at[0]),
        pltpu.make_async_copy(pre_h, pre_v, in_sem.at[1]),
        pltpu.make_async_copy(up_h, up_v, in_sem.at[2]),
        pltpu.make_async_copy(weight_h, w_v, in_sem.at[3]),
        pltpu.make_async_copy(rows_h, rows_v, in_sem.at[4]),
        pltpu.make_async_copy(cols_h, cols_v, in_sem.at[6]),
        pltpu.make_async_copy(count_h, count, in_sem.at[7]),
        pltpu.make_async_copy(adj_h, a_v.at[pl.ds(0, slots)], in_sem.at[5]),
    ]
    for load in loads:
        load.start()
    a_v[slots] = jnp.zeros((BLK, BLK), jnp.bfloat16)
    acc[...] = jnp.zeros_like(acc)
    for load in loads[:-1]:
        load.wait()
    grad_pre = jnp.where(
        pre_v[...].astype(jnp.float32) > 0, up_v[...].astype(jnp.float32), 0.0
    )
    pair = x * 2 + y_lo
    g_v[core, pair] = grad_pre.T.astype(jnp.bfloat16)
    grad_out[...] = lax.dot_general(
        grad_pre.astype(jnp.bfloat16),
        w_v[...],
        (((1,), (1,)), ((), ())),
        preferred_element_type=jnp.float32,
    ).astype(jnp.bfloat16)

    lane = lax.broadcasted_iota(jnp.int32, (1, slots), 1)
    place = jnp.where(lane < count[0, 0], cols_v[...] * NC + rows_v[...], -1)
    places = jnp.broadcast_to(place, (slots, slots)).T
    behind = lax.broadcasted_iota(jnp.int32, (slots, BLK), 0) - slots
    wanted = lax.broadcasted_iota(jnp.int32, (slots, BLK), 1)
    for k in range(NR * NC // BLK):
        hit = places == wanted + k * BLK
        table_v[k : k + 1, :] = slots + jnp.sum(
            jnp.where(hit, behind, 0), axis=0, keepdims=True
        )
    to_scalars = pltpu.make_async_copy(table_v, table, in_sem.at[4])
    to_scalars.start()

    pl.semaphore_wait(barrier, len(hello))

    def forward(b, to, j, d):
        pltpu.make_async_remote_copy(
            src_ref=x_v.at[b],
            dst_ref=x_v.at[b],
            send_sem=x_send,
            recv_sem=x_recv.at[j * NZ + d],
            device_id=(to, col),
            device_id_type=MESH,
        ).start()

    def arrived(j, d):
        b = at(j, d)
        pltpu.make_async_copy(x_v.at[b], x_v.at[b], x_recv.at[j * NZ + d]).wait()

    for j in (2, 1, 3):
        forward(row, at(NY - j, 0), j, 0)
    for d in Z_ORDER:
        forward(row, at(0, NZ - d), 0, d)
    for i in range(NX):
        for m in range(2):
            if i or m:
                pltpu.make_async_remote_copy(
                    src_ref=g_v.at[core, pair],
                    dst_ref=g_v.at[core, pair],
                    send_sem=g_sem.at[0],
                    recv_sem=g_sem.at[1],
                    device_id=(row, over(i, m, 0)),
                    device_id_type=MESH,
                ).start()

    for j in (1, 3):
        arrived(j, 0)
        for d in NEAR[j]:
            forward(at(j, 0), at(0, NZ - d), j, d)
    for d in FAR[:2]:
        arrived(0, d)
        for j in (1, 3, 2):
            if d not in NEAR[j]:
                forward(at(0, d), at(NY - j, 0), j, d)
    arrived(2, 0)
    for d in NEAR[2]:
        forward(at(2, 0), at(0, NZ - d), 2, d)
    arrived(0, 4)
    for j in (1, 3, 2):
        forward(at(0, 4), at(NY - j, 0), j, 4)
    to_scalars.wait()
    loads[-1].wait()

    def multiply(blocks):
        tiles = jnp.concatenate([x_v[b] for b in blocks], axis=0)
        for g in range(NC // GROUP):
            lhs = jnp.concatenate(
                [
                    jnp.concatenate(
                        [a_v[table[b // 8, b % 8 * NC + r]] for b in blocks], axis=1
                    )
                    for r in range(g * GROUP, (g + 1) * GROUP)
                ],
                axis=0,
            )
            span = pl.ds(g * GROUP * BLK, GROUP * BLK)
            acc[span, :] += jnp.dot(lhs, tiles, preferred_element_type=jnp.float32)

    all_g = g_v.at[0, pl.ds(0, NQ - 1)]
    sibling = pltpu.make_async_remote_copy(
        src_ref=g_v.at[core],
        dst_ref=g_v.at[core],
        send_sem=g_sem.at[2],
        recv_sem=g_sem.at[3],
        device_id=(row, over(0, 0, 1)),
        device_id_type=MESH,
    )

    def step(o, _):
        d = jnp.where(o % 2 == 1, (o + 1) // 2, (NZ - o // 2) % NZ)

        @pl.when(o > 0)
        def _():
            @pl.when((d < 3) | (d > 5))
            def _():
                arrived(0, d)

            for j in (1, 3, 2):
                arrived(j, d)

        @pl.when(o == 2)
        def _():
            pltpu.make_async_copy(all_g, all_g, g_sem.at[1]).wait()
            sibling.start()

        multiply([at(j, d) for j in range(NY)])
        return 0

    lax.fori_loop(0, NZ, step, 0)

    sibling.wait_recv()
    part[...] = acc[...].reshape(NC, BLK, BLK).astype(jnp.bfloat16)
    term = jnp.zeros((BLK, BLK), jnp.float32)
    for i in range(NQ):
        term = term + jnp.dot(
            jnp.concatenate([g_v[0, i], g_v[1, i]], axis=1),
            part[2 * i : 2 * i + 2].reshape(2 * BLK, BLK),
            preferred_element_type=jnp.float32,
        )
    w_loc[...] = term.reshape(NQ, SLICE, BLK)

    q = x * 2 + core
    y_at = y * 2 + y_lo
    q_peers = [(i, c) for i in (2, 1, 3, 0) for c in range(2) if i or c]

    def slot_of(i, c):
        return wrap(x + i, NX) * 2 + wrap(core + c, 2)

    def send(src, dst, k, peer):
        pltpu.make_async_remote_copy(
            src_ref=src,
            dst_ref=dst,
            send_sem=w_sem.at[2 * k],
            recv_sem=w_sem.at[2 * k + 1],
            device_id=peer,
            device_id_type=MESH,
        ).start()

    def total(buf):
        t = buf[0]
        for k in range(1, buf.shape[0]):
            t = t + buf[k]
        return t

    def seven(buf, sem):
        some = buf.at[pl.ds(0, 7)]
        pltpu.make_async_copy(some, some, sem).wait()

    for i, c in q_peers:
        send(w_loc.at[slot_of(i, c)], w_in1.at[q], 0, (row, over(i, 0, c)))
    w_in1[q] = w_loc[q]
    seven(w_in1, w_sem.at[1])
    mid = total(w_in1)
    w_my[...] = mid
    for peer in y_peers:
        send(w_my, w_iny.at[y_at], 1, peer)
    w_iny[y_at] = mid

    for k in range(1, NC):
        to = wrap(col + k, NC)
        pltpu.make_async_remote_copy(
            src_ref=part.at[to],
            dst_ref=parts_in.at[NC - 1 - k],
            send_sem=r_sem.at[0],
            recv_sem=r_sem.at[1],
            device_id=(row, to),
            device_id_type=MESH,
        ).start()

    seven(w_iny, w_sem.at[3])
    mid = total(w_iny)
    w_mz[...] = mid
    for peer in z_peers:
        send(w_mz, w_inz.at[z], 2, peer)
    w_inz[z] = mid

    whole = parts_in.at[pl.ds(0, NC - 1)]
    pltpu.make_async_copy(whole, whole, r_sem.at[1]).wait()
    mine = acc[pl.ds(pl.multiple_of(col * BLK, BLK), BLK), :]
    for k in range(NC - 1):
        mine = mine + parts_in[k].astype(jnp.float32)
    agg_out[...] = mine.astype(jnp.bfloat16)

    seven(w_inz, w_sem.at[5])
    w_fin[q] = total(w_inz) * scale
    for i, c in q_peers:
        send(w_fin.at[q], w_fin.at[q], 3, (row, over(i, 0, c)))
    seven(w_fin, w_sem.at[7])
    wg_out[...] = w_fin[...].reshape(BLK, BLK).T

    most = x_v.at[pl.ds(0, NR - 1)]
    pltpu.make_async_copy(most, most, x_send).wait()
    pltpu.make_async_copy(all_g, all_g, g_sem.at[0]).wait()
    sibling.wait_send()
    pltpu.make_async_copy(whole, whole, r_sem.at[0]).wait()
    for k, buf in enumerate((w_in1, w_iny, w_inz, w_fin)):
        seven(buf, w_sem.at[2 * k])


def finish(agg, wg, grad, agg_out, wg_out, grad_out):
    agg_out[...] = agg[...]
    wg_out[...] = wg[...]
    grad_out[...] = grad[...]


def per_device(
    features, adj_blocks, block_rows, block_cols, block_counts, weight, pre_act, upstream
):
    blocks = adj_blocks[0, 0]
    slots = blocks.shape[0]
    vmem = pl.BlockSpec(memory_space=pltpu.VMEM)
    hbm = pl.BlockSpec(memory_space=pltpu.HBM)
    bf16, f32 = jnp.bfloat16, jnp.float32
    nodes = BLK * NR * NC
    wide = (8, SLICE, BLK)
    dma = pltpu.SemaphoreType.DMA
    results = pl.pallas_call(
        functools.partial(kernel, 1.0 / math.sqrt(nodes)),
        out_shape=(
            jax.ShapeDtypeStruct((BLK, BLK), bf16),
            jax.ShapeDtypeStruct((BLK, BLK), f32),
            jax.ShapeDtypeStruct((BLK, BLK), bf16),
        ),
        in_specs=[hbm] * 8,
        out_specs=(vmem, vmem, vmem),
        scratch_shapes=[
            pltpu.SMEM((NR * NC // BLK, BLK), jnp.int32),
            pltpu.VMEM((NR * NC // BLK, BLK), jnp.int32),
            pltpu.VMEM((1, slots), jnp.int32),
            pltpu.VMEM((1, slots), jnp.int32),
            pltpu.SMEM((1, 1), jnp.int32),
            pltpu.VMEM((BLK, BLK), bf16),
            pltpu.VMEM((BLK, BLK), bf16),
            pltpu.VMEM((BLK, BLK), bf16),
            pltpu.VMEM((slots + 1, BLK, BLK), bf16),
            pltpu.VMEM((NR, BLK, BLK), bf16),
            pltpu.VMEM((2, NQ, BLK, BLK), bf16),
            pltpu.VMEM((ROWS, BLK), f32),
            pltpu.VMEM((NC, BLK, BLK), bf16),
            pltpu.VMEM((NC, BLK, BLK), bf16),
            pltpu.VMEM(wide, f32),
            pltpu.VMEM(wide, f32),
            pltpu.VMEM((SLICE, BLK), f32),
            pltpu.VMEM(wide, f32),
            pltpu.VMEM((SLICE, BLK), f32),
            pltpu.VMEM(wide, f32),
            pltpu.VMEM(wide, f32),
            dma((8,)),
            dma,
            dma((NR,)),
            dma((4,)),
            dma((2,)),
            dma((8,)),
        ],
        compiler_params=pltpu.CompilerParams(
            collective_id=0, has_side_effects=True, vmem_limit_bytes=VMEM_BYTES
        ),
        name="gcn",
    )(
        block_rows[0],
        block_cols[0],
        block_counts,
        features,
        blocks,
        weight,
        pre_act,
        upstream,
    )
    return pl.pallas_call(
        finish,
        out_shape=tuple(jax.ShapeDtypeStruct(r.shape, r.dtype) for r in results),
        in_specs=[vmem] * 3,
        out_specs=(vmem, vmem, vmem),
        compiler_params=pltpu.CompilerParams(vmem_limit_bytes=VMEM_BYTES),
        name="finish",
    )(*results)


def solution(mesh):
    placed = (
        P(("col", "row"), None),
        P("row", "col", None, None, None),
        P("row", "col", None),
        P("row", "col", None),
        P("row", "col"),
        P(),
        P(("row", "col"), None),
        P(("row", "col"), None),
    )
    return jax.shard_map(
        per_device,
        mesh=mesh,
        in_specs=placed,
        out_specs=(P(("row", "col"), None), P(), P(("row", "col"), None)),
        check_vma=False,
    )
```

```python
import functools
import math

import jax
import jax.numpy as jnp
from jax import lax
from jax.experimental import pallas as pl
from jax.experimental.pallas import tpu as pltpu
from jax.sharding import PartitionSpec as P

MESH = pl.DeviceIdType.MESH
NY = 4
NZ = 8
NR = NY * NZ
NX = 4
NC = 16
NQ = NX * 2
BLK = 128
ROWS = NC * BLK
VMEM_BYTES = 63 * 1024 * 1024
GROUP = 2
SLICE = BLK // NQ
NEAR = ((), (1, 7, 2, 6), (1, 7, 2, 6, 3), (1, 7, 2, 6))
FAR = (3, 5, 4)
Z_ORDER = (4, 3, 5, 2, 6, 1, 7)


def wrap(t, n):
    return jnp.where(t >= n, t - n, t)


def kernel(
    scale,
    rows_h,
    cols_h,
    count_h,
    feat_h,
    adj_h,
    weight_h,
    pre_h,
    up_h,
    agg_out,
    wg_out,
    grad_out,
    table,
    table_v,
    rows_v,
    cols_v,
    count,
    w_v,
    pre_v,
    up_v,
    a_v,
    x_v,
    g_v,
    h_v,
    acc,
    part,
    parts_in,
    w_loc,
    w_in1,
    w_my,
    w_iny,
    w_mz,
    w_inz,
    w_fin,
    in_sem,
    x_send,
    x_recv,
    g_sem,
    r_sem,
    w_sem,
):
    row = lax.axis_index("row")
    col = lax.axis_index("col")
    y = row // NZ
    z = row - y * NZ
    x = col // 4
    y_lo = (col // 2) % 2
    core = col % 2
    slots = adj_h.shape[0]

    def at(j, d):
        return wrap(y + j, NY) * NZ + wrap(z + d, NZ)

    def over(i, m, c):
        return wrap(x + i, NX) * 4 + wrap(y_lo + m, 2) * 2 + wrap(core + c, 2)

    z_peers = [(at(0, d), col) for d in Z_ORDER]
    y_peers = [
        (at(j, 0), over(0, m, 0)) for j in (2, 1, 3, 0) for m in range(2) if j or m
    ]
    col_peers = [
        (row, over(i, m, c))
        for i in (2, 1, 3, 0)
        for m in range(2)
        for c in range(2)
        if i or m or c
    ]
    far_y = [(at(j, 0), over(0, 1, 0)) for j in (2, 1, 3)]
    near_y = [(at(j, 0), col) for j in (2, 1, 3)]

    barrier = pltpu.get_barrier_semaphore()
    hello = z_peers + near_y + far_y + col_peers
    for peer in hello:
        pl.semaphore_signal(barrier, inc=1, device_id=peer, device_id_type=MESH)

    loads = [
        pltpu.make_async_copy(feat_h, x_v.at[row], in_sem.at[0]),
        pltpu.make_async_copy(pre_h, pre_v, in_sem.at[1]),
        pltpu.make_async_copy(up_h, up_v, in_sem.at[2]),
        pltpu.make_async_copy(weight_h, w_v, in_sem.at[3]),
        pltpu.make_async_copy(rows_h, rows_v, in_sem.at[4]),
        pltpu.make_async_copy(cols_h, cols_v, in_sem.at[6]),
        pltpu.make_async_copy(count_h, count, in_sem.at[7]),
        pltpu.make_async_copy(adj_h, a_v.at[pl.ds(0, slots)], in_sem.at[5]),
    ]
    for load in loads:
        load.start()
    pl.semaphore_wait(barrier, len(hello))

    def forward(b, to, j, d, src=None):
        pltpu.make_async_remote_copy(
            src_ref=x_v.at[b] if src is None else src,
            dst_ref=x_v.at[b],
            send_sem=x_send,
            recv_sem=x_recv.at[j * NZ + d],
            device_id=(to, col),
            device_id_type=MESH,
        ).start()

    def arrived(j, d):
        b = at(j, d)
        pltpu.make_async_copy(x_v.at[b], x_v.at[b], x_recv.at[j * NZ + d]).wait()

    for j in (2, 1, 3):
        forward(row, at(NY - j, 0), j, 0, feat_h)
    for d in Z_ORDER:
        forward(row, at(0, NZ - d), 0, d, feat_h)
    a_v[slots] = jnp.zeros((BLK, BLK), jnp.bfloat16)
    acc[...] = jnp.zeros_like(acc)
    for load in loads[:-1]:
        load.wait()
    grad_pre = jnp.where(
        pre_v[...].astype(jnp.float32) > 0, up_v[...].astype(jnp.float32), 0.0
    )
    pair = x * 2 + y_lo
    g_v[core, pair] = grad_pre.T.astype(jnp.bfloat16)
    grad_out[...] = lax.dot_general(
        grad_pre.astype(jnp.bfloat16),
        w_v[...],
        (((1,), (1,)), ((), ())),
        preferred_element_type=jnp.float32,
    ).astype(jnp.bfloat16)

    lane = lax.broadcasted_iota(jnp.int32, (1, slots), 1)
    place = jnp.where(lane < count[0, 0], cols_v[...] * NC + rows_v[...], -1)
    places = jnp.broadcast_to(place, (slots, slots)).T
    behind = lax.broadcasted_iota(jnp.int32, (slots, BLK), 0) - slots
    wanted = lax.broadcasted_iota(jnp.int32, (slots, BLK), 1)
    for k in range(NR * NC // BLK):
        hit = places == wanted + k * BLK
        table_v[k : k + 1, :] = slots + jnp.sum(
            jnp.where(hit, behind, 0), axis=0, keepdims=True
        )
    to_scalars = pltpu.make_async_copy(table_v, table, in_sem.at[4])
    to_scalars.start()

    for i in range(NX):
        for m in range(2):
            if i or m:
                pltpu.make_async_remote_copy(
                    src_ref=g_v.at[core, pair],
                    dst_ref=g_v.at[core, pair],
                    send_sem=g_sem.at[0],
                    recv_sem=g_sem.at[1],
                    device_id=(row, over(i, m, 0)),
                    device_id_type=MESH,
                ).start()

    for j in (1, 3):
        arrived(j, 0)
        for d in NEAR[j]:
            forward(at(j, 0), at(0, NZ - d), j, d)
    for d in FAR[:2]:
        arrived(0, d)
        for j in (1, 3, 2):
            if d not in NEAR[j]:
                forward(at(0, d), at(NY - j, 0), j, d)
    arrived(2, 0)
    for d in NEAR[2]:
        forward(at(2, 0), at(0, NZ - d), 2, d)
    arrived(0, 4)
    for j in (1, 3, 2):
        forward(at(0, 4), at(NY - j, 0), j, 4)
    to_scalars.wait()
    loads[-1].wait()

    def slot(b, r):
        return table[b // 8, b % 8 * NC + r]

    def multiply(blocks):
        tiles = jnp.concatenate([x_v[b] for b in blocks], axis=0)
        for g in range(NC // GROUP):
            lhs = jnp.concatenate(
                [
                    jnp.concatenate(
                        [a_v[slot(b, r)] for b in blocks], axis=1
                    )
                    for r in range(g * GROUP, (g + 1) * GROUP)
                ],
                axis=0,
            )
            span = pl.ds(g * GROUP * BLK, GROUP * BLK)
            acc[span, :] += jnp.dot(lhs, tiles, preferred_element_type=jnp.float32)

    all_g = g_v.at[0, pl.ds(0, NQ - 1)]
    sibling = pltpu.make_async_remote_copy(
        src_ref=g_v.at[core],
        dst_ref=g_v.at[core],
        send_sem=g_sem.at[2],
        recv_sem=g_sem.at[3],
        device_id=(row, over(0, 0, 1)),
        device_id_type=MESH,
    )

    def z_step(o):
        return jnp.where(o % 2 == 1, (o + 1) // 2, (NZ - o // 2) % NZ)

    def step(o, _):
        multiply([at(j, z_step(o)) for j in range(NY)])
        return 0

    def pull(k, _):
        lhs = jnp.concatenate([g_v[i % 2, i // 2] for i in range(NC)], axis=1)
        rhs = jnp.concatenate(
            [
                jnp.concatenate([a_v[slot(2 * k, r)], a_v[slot(2 * k + 1, r)]], axis=1)
                for r in range(NC)
            ],
            axis=0,
        )
        pulled = jnp.dot(lhs, rhs, preferred_element_type=jnp.float32).astype(jnp.bfloat16)
        h_v[2 * k] = pulled[:, :BLK]
        h_v[2 * k + 1] = pulled[:, BLK:]
        return 0

    def add_term(o, term):
        d = z_step(o)

        @pl.when(o > 0)
        def _():
            @pl.when((d < 3) | (d > 5))
            def _():
                arrived(0, d)

            for j in (1, 3, 2):
                arrived(j, d)

        blocks = [at(j, d) for j in range(NY)]
        return term + jnp.dot(
            jnp.concatenate([h_v[b] for b in blocks], axis=1),
            jnp.concatenate([x_v[b] for b in blocks], axis=0),
            preferred_element_type=jnp.float32,
        )

    pltpu.make_async_copy(all_g, all_g, g_sem.at[1]).wait()
    sibling.start()
    lax.fori_loop(0, 1, step, 0)
    sibling.wait_recv()
    lax.fori_loop(0, NR // 2, pull, 0)
    term = lax.fori_loop(0, NZ, add_term, jnp.zeros((BLK, BLK), jnp.float32))
    w_loc[...] = term.reshape(NQ, SLICE, BLK)

    q = x * 2 + core
    y_at = y * 2 + y_lo
    q_peers = [(i, c) for i in (2, 1, 3, 0) for c in range(2) if i or c]

    def slot_of(i, c):
        return wrap(x + i, NX) * 2 + wrap(core + c, 2)

    def send(src, dst, k, peer):
        pltpu.make_async_remote_copy(
            src_ref=src,
            dst_ref=dst,
            send_sem=w_sem.at[2 * k],
            recv_sem=w_sem.at[2 * k + 1],
            device_id=peer,
            device_id_type=MESH,
        ).start()

    def total(buf):
        t = buf[0]
        for k in range(1, buf.shape[0]):
            t = t + buf[k]
        return t

    def seven(buf, sem):
        some = buf.at[pl.ds(0, 7)]
        pltpu.make_async_copy(some, some, sem).wait()

    for i, c in q_peers:
        send(w_loc.at[slot_of(i, c)], w_in1.at[q], 0, (row, over(i, 0, c)))
    w_in1[q] = w_loc[q]
    lax.fori_loop(1, 5, step, 0)
    seven(w_in1, w_sem.at[1])
    mid = total(w_in1)
    w_my[...] = mid
    for peer in y_peers:
        send(w_my, w_iny.at[y_at], 1, peer)
    w_iny[y_at] = mid

    lax.fori_loop(5, NZ, step, 0)
    part[...] = acc[...].reshape(NC, BLK, BLK).astype(jnp.bfloat16)
    for k in range(1, NC):
        to = wrap(col + k, NC)
        pltpu.make_async_remote_copy(
            src_ref=part.at[to],
            dst_ref=parts_in.at[NC - 1 - k],
            send_sem=r_sem.at[0],
            recv_sem=r_sem.at[1],
            device_id=(row, to),
            device_id_type=MESH,
        ).start()

    seven(w_iny, w_sem.at[3])
    mid = total(w_iny)
    w_mz[...] = mid
    for peer in z_peers:
        send(w_mz, w_inz.at[z], 2, peer)
    w_inz[z] = mid

    whole = parts_in.at[pl.ds(0, NC - 1)]
    pltpu.make_async_copy(whole, whole, r_sem.at[1]).wait()
    mine = acc[pl.ds(pl.multiple_of(col * BLK, BLK), BLK), :]
    for k in range(NC - 1):
        mine = mine + parts_in[k].astype(jnp.float32)
    agg_out[...] = mine.astype(jnp.bfloat16)

    seven(w_inz, w_sem.at[5])
    w_fin[q] = total(w_inz) * scale
    for i, c in q_peers:
        send(w_fin.at[q], w_fin.at[q], 3, (row, over(i, 0, c)))
    seven(w_fin, w_sem.at[7])
    wg_out[...] = w_fin[...].reshape(BLK, BLK).T

    most = x_v.at[pl.ds(0, NR - 1)]
    pltpu.make_async_copy(most, most, x_send).wait()
    pltpu.make_async_copy(all_g, all_g, g_sem.at[0]).wait()
    sibling.wait_send()
    pltpu.make_async_copy(whole, whole, r_sem.at[0]).wait()
    for k, buf in enumerate((w_in1, w_iny, w_inz, w_fin)):
        seven(buf, w_sem.at[2 * k])


def finish(agg, wg, grad, agg_out, wg_out, grad_out):
    agg_out[...] = agg[...]
    wg_out[...] = wg[...]
    grad_out[...] = grad[...]


def per_device(
    features, adj_blocks, block_rows, block_cols, block_counts, weight, pre_act, upstream
):
    blocks = adj_blocks[0, 0]
    slots = blocks.shape[0]
    vmem = pl.BlockSpec(memory_space=pltpu.VMEM)
    hbm = pl.BlockSpec(memory_space=pltpu.HBM)
    bf16, f32 = jnp.bfloat16, jnp.float32
    nodes = BLK * NR * NC
    wide = (8, SLICE, BLK)
    dma = pltpu.SemaphoreType.DMA
    results = pl.pallas_call(
        functools.partial(kernel, 1.0 / math.sqrt(nodes)),
        out_shape=(
            jax.ShapeDtypeStruct((BLK, BLK), bf16),
            jax.ShapeDtypeStruct((BLK, BLK), f32),
            jax.ShapeDtypeStruct((BLK, BLK), bf16),
        ),
        in_specs=[hbm] * 8,
        out_specs=(vmem, vmem, vmem),
        scratch_shapes=[
            pltpu.SMEM((NR * NC // BLK, BLK), jnp.int32),
            pltpu.VMEM((NR * NC // BLK, BLK), jnp.int32),
            pltpu.VMEM((1, slots), jnp.int32),
            pltpu.VMEM((1, slots), jnp.int32),
            pltpu.SMEM((1, 1), jnp.int32),
            pltpu.VMEM((BLK, BLK), bf16),
            pltpu.VMEM((BLK, BLK), bf16),
            pltpu.VMEM((BLK, BLK), bf16),
            pltpu.VMEM((slots + 1, BLK, BLK), bf16),
            pltpu.VMEM((NR, BLK, BLK), bf16),
            pltpu.VMEM((2, NQ, BLK, BLK), bf16),
            pltpu.VMEM((NR, BLK, BLK), bf16),
            pltpu.VMEM((ROWS, BLK), f32),
            pltpu.VMEM((NC, BLK, BLK), bf16),
            pltpu.VMEM((NC, BLK, BLK), bf16),
            pltpu.VMEM(wide, f32),
            pltpu.VMEM(wide, f32),
            pltpu.VMEM((SLICE, BLK), f32),
            pltpu.VMEM(wide, f32),
            pltpu.VMEM((SLICE, BLK), f32),
            pltpu.VMEM(wide, f32),
            pltpu.VMEM(wide, f32),
            dma((8,)),
            dma,
            dma((NR,)),
            dma((4,)),
            dma((2,)),
            dma((8,)),
        ],
        compiler_params=pltpu.CompilerParams(
            collective_id=0, has_side_effects=True, vmem_limit_bytes=VMEM_BYTES
        ),
        name="gcn",
    )(
        block_rows[0],
        block_cols[0],
        block_counts,
        features,
        blocks,
        weight,
        pre_act,
        upstream,
    )
    return pl.pallas_call(
        finish,
        out_shape=tuple(jax.ShapeDtypeStruct(r.shape, r.dtype) for r in results),
        in_specs=[vmem] * 3,
        out_specs=(vmem, vmem, vmem),
        compiler_params=pltpu.CompilerParams(vmem_limit_bytes=VMEM_BYTES),
        name="finish",
    )(*results)


def solution(mesh):
    placed = (
        P(("col", "row"), None),
        P("row", "col", None, None, None),
        P("row", "col", None),
        P("row", "col", None),
        P("row", "col"),
        P(),
        P(("row", "col"), None),
        P(("row", "col"), None),
    )
    return jax.shard_map(
        per_device,
        mesh=mesh,
        in_specs=placed,
        out_specs=(P(("row", "col"), None), P(), P(("row", "col"), None)),
        check_vma=False,
    )
```

```python
import functools
import math

import jax
import jax.numpy as jnp
from jax import lax
from jax.experimental import pallas as pl
from jax.experimental.pallas import tpu as pltpu
from jax.sharding import PartitionSpec as P

MESH = pl.DeviceIdType.MESH
NY = 4
NZ = 8
NR = NY * NZ
NX = 4
NC = 16
NQ = NX * 2
BLK = 128
ROWS = NC * BLK
VMEM_BYTES = 63 * 1024 * 1024
GROUP = 2
SLICE = BLK // NQ
NEAR = ((), (1, 7, 2, 6), (1, 7, 2, 6, 3), (1, 7, 2, 6))
FAR = (3, 5, 4)
Z_ORDER = (4, 3, 5, 2, 6, 1, 7)


def wrap(t, n):
    return jnp.where(t >= n, t - n, t)


def kernel(
    scale,
    rows_h,
    cols_h,
    count_h,
    feat_h,
    adj_h,
    weight_h,
    pre_h,
    up_h,
    agg_out,
    wg_out,
    grad_out,
    table,
    table_v,
    rows_v,
    cols_v,
    count,
    w_v,
    pre_v,
    up_v,
    a_v,
    x_v,
    g_v,
    h_v,
    acc,
    part,
    parts_in,
    w_loc,
    w_in1,
    w_my,
    w_iny,
    w_mz,
    w_inz,
    w_fin,
    in_sem,
    x_send,
    x_recv,
    g_sem,
    r_sem,
    w_sem,
):
    row = lax.axis_index("row")
    col = lax.axis_index("col")
    y = row // NZ
    z = row - y * NZ
    x = col // 4
    y_lo = (col // 2) % 2
    core = col % 2
    slots = adj_h.shape[0]

    def at(j, d):
        return wrap(y + j, NY) * NZ + wrap(z + d, NZ)

    def over(i, m, c):
        return wrap(x + i, NX) * 4 + wrap(y_lo + m, 2) * 2 + wrap(core + c, 2)

    z_peers = [(at(0, d), col) for d in Z_ORDER]
    y_peers = [
        (at(j, 0), over(0, m, 0)) for j in (2, 1, 3, 0) for m in range(2) if j or m
    ]
    col_peers = [
        (row, over(i, m, c))
        for i in (2, 1, 3, 0)
        for m in range(2)
        for c in range(2)
        if i or m or c
    ]
    far_y = [(at(j, 0), over(0, 1, 0)) for j in (2, 1, 3)]
    near_y = [(at(j, 0), col) for j in (2, 1, 3)]

    barrier = pltpu.get_barrier_semaphore()
    hello = z_peers + near_y + far_y + col_peers
    for peer in hello:
        pl.semaphore_signal(barrier, inc=1, device_id=peer, device_id_type=MESH)

    loads = [
        pltpu.make_async_copy(feat_h, x_v.at[row], in_sem.at[0]),
        pltpu.make_async_copy(pre_h, pre_v, in_sem.at[1]),
        pltpu.make_async_copy(up_h, up_v, in_sem.at[2]),
        pltpu.make_async_copy(weight_h, w_v, in_sem.at[3]),
        pltpu.make_async_copy(rows_h, rows_v, in_sem.at[4]),
        pltpu.make_async_copy(cols_h, cols_v, in_sem.at[6]),
        pltpu.make_async_copy(count_h, count, in_sem.at[7]),
        pltpu.make_async_copy(adj_h, a_v.at[pl.ds(0, slots)], in_sem.at[5]),
    ]
    for load in loads:
        load.start()
    pl.semaphore_wait(barrier, len(hello))

    def forward(b, to, j, d, src=None):
        pltpu.make_async_remote_copy(
            src_ref=x_v.at[b] if src is None else src,
            dst_ref=x_v.at[b],
            send_sem=x_send,
            recv_sem=x_recv.at[j * NZ + d],
            device_id=(to, col),
            device_id_type=MESH,
        ).start()

    def arrived(j, d):
        b = at(j, d)
        pltpu.make_async_copy(x_v.at[b], x_v.at[b], x_recv.at[j * NZ + d]).wait()

    for j in (2, 1, 3):
        forward(row, at(NY - j, 0), j, 0, feat_h)
    for d in Z_ORDER:
        forward(row, at(0, NZ - d), 0, d, feat_h)
    a_v[slots] = jnp.zeros((BLK, BLK), jnp.bfloat16)
    acc[...] = jnp.zeros_like(acc)
    for load in loads[:-1]:
        load.wait()
    grad_pre = jnp.where(
        pre_v[...].astype(jnp.float32) > 0, up_v[...].astype(jnp.float32), 0.0
    )
    pair = x * 2 + y_lo
    g_v[core, pair] = grad_pre.T.astype(jnp.bfloat16)
    grad_out[...] = lax.dot_general(
        grad_pre.astype(jnp.bfloat16),
        w_v[...],
        (((1,), (1,)), ((), ())),
        preferred_element_type=jnp.float32,
    ).astype(jnp.bfloat16)

    lane = lax.broadcasted_iota(jnp.int32, (1, slots), 1)
    place = jnp.where(lane < count[0, 0], cols_v[...] * NC + rows_v[...], -1)
    places = jnp.broadcast_to(place, (slots, slots)).T
    behind = lax.broadcasted_iota(jnp.int32, (slots, BLK), 0) - slots
    wanted = lax.broadcasted_iota(jnp.int32, (slots, BLK), 1)
    for k in range(NR * NC // BLK):
        hit = places == wanted + k * BLK
        table_v[k : k + 1, :] = slots + jnp.sum(
            jnp.where(hit, behind, 0), axis=0, keepdims=True
        )
    to_scalars = pltpu.make_async_copy(table_v, table, in_sem.at[4])
    to_scalars.start()

    for i in range(NX):
        for m in range(2):
            if i or m:
                pltpu.make_async_remote_copy(
                    src_ref=g_v.at[core, pair],
                    dst_ref=g_v.at[core, pair],
                    send_sem=g_sem.at[0],
                    recv_sem=g_sem.at[1],
                    device_id=(row, over(i, m, 0)),
                    device_id_type=MESH,
                ).start()

    for j in (1, 3):
        arrived(j, 0)
        for d in NEAR[j]:
            forward(at(j, 0), at(0, NZ - d), j, d)
    for d in FAR[:2]:
        arrived(0, d)
        for j in (2, 1, 3):
            if d not in NEAR[j]:
                forward(at(0, d), at(NY - j, 0), j, d)
    arrived(2, 0)
    for d in NEAR[2]:
        forward(at(2, 0), at(0, NZ - d), 2, d)
    arrived(0, 4)
    for j in (2, 1, 3):
        forward(at(0, 4), at(NY - j, 0), j, 4)
    to_scalars.wait()
    loads[-1].wait()

    def slot(b, r):
        return table[b // 8, b % 8 * NC + r]

    def multiply(blocks):
        tiles = jnp.concatenate([x_v[b] for b in blocks], axis=0)
        for g in range(NC // GROUP):
            lhs = jnp.concatenate(
                [
                    jnp.concatenate(
                        [a_v[slot(b, r)] for b in blocks], axis=1
                    )
                    for r in range(g * GROUP, (g + 1) * GROUP)
                ],
                axis=0,
            )
            span = pl.ds(g * GROUP * BLK, GROUP * BLK)
            acc[span, :] += jnp.dot(lhs, tiles, preferred_element_type=jnp.float32)

    all_g = g_v.at[0, pl.ds(0, NQ - 1)]
    sibling = pltpu.make_async_remote_copy(
        src_ref=g_v.at[core],
        dst_ref=g_v.at[core],
        send_sem=g_sem.at[2],
        recv_sem=g_sem.at[3],
        device_id=(row, over(0, 0, 1)),
        device_id_type=MESH,
    )

    def z_step(o):
        return jnp.where(o % 2 == 1, (o + 1) // 2, (NZ - o // 2) % NZ)

    def step(o, _):
        multiply([at(j, z_step(o)) for j in range(NY)])
        return 0

    def pull(k, _):
        lhs = jnp.concatenate([g_v[i % 2, i // 2] for i in range(NC)], axis=1)
        rhs = jnp.concatenate(
            [
                jnp.concatenate([a_v[slot(2 * k, r)], a_v[slot(2 * k + 1, r)]], axis=1)
                for r in range(NC)
            ],
            axis=0,
        )
        pulled = jnp.dot(lhs, rhs, preferred_element_type=jnp.float32).astype(jnp.bfloat16)
        h_v[2 * k] = pulled[:, :BLK]
        h_v[2 * k + 1] = pulled[:, BLK:]
        return 0

    def add_term(o, term):
        d = z_step(o)

        @pl.when(o > 0)
        def _():
            @pl.when((d < 3) | (d > 5))
            def _():
                arrived(0, d)

            for j in (1, 3, 2):
                arrived(j, d)

        blocks = [at(j, d) for j in range(NY)]
        return term + jnp.dot(
            jnp.concatenate([h_v[b] for b in blocks], axis=1),
            jnp.concatenate([x_v[b] for b in blocks], axis=0),
            preferred_element_type=jnp.float32,
        )

    pltpu.make_async_copy(all_g, all_g, g_sem.at[1]).wait()
    sibling.start()
    lax.fori_loop(0, 1, step, 0)
    sibling.wait_recv()
    lax.fori_loop(0, NR // 2, pull, 0)
    term = lax.fori_loop(0, NZ, add_term, jnp.zeros((BLK, BLK), jnp.float32))
    w_loc[...] = term.reshape(NQ, SLICE, BLK)

    q = x * 2 + core
    y_at = y * 2 + y_lo
    q_peers = [(i, c) for i in (2, 1, 3, 0) for c in range(2) if i or c]

    def slot_of(i, c):
        return wrap(x + i, NX) * 2 + wrap(core + c, 2)

    def send(src, dst, k, peer):
        pltpu.make_async_remote_copy(
            src_ref=src,
            dst_ref=dst,
            send_sem=w_sem.at[2 * k],
            recv_sem=w_sem.at[2 * k + 1],
            device_id=peer,
            device_id_type=MESH,
        ).start()

    def total(buf):
        t = buf[0]
        for k in range(1, buf.shape[0]):
            t = t + buf[k]
        return t

    def seven(buf, sem):
        some = buf.at[pl.ds(0, 7)]
        pltpu.make_async_copy(some, some, sem).wait()

    for i, c in q_peers:
        send(w_loc.at[slot_of(i, c)], w_in1.at[q], 0, (row, over(i, 0, c)))
    w_in1[q] = w_loc[q]
    lax.fori_loop(1, 5, step, 0)
    seven(w_in1, w_sem.at[1])
    mid = total(w_in1)
    w_my[...] = mid
    for peer in y_peers:
        send(w_my, w_iny.at[y_at], 1, peer)
    w_iny[y_at] = mid

    lax.fori_loop(5, NZ, step, 0)
    part[...] = acc[...].reshape(NC, BLK, BLK).astype(jnp.bfloat16)
    for k in range(1, NC):
        to = wrap(col + k, NC)
        pltpu.make_async_remote_copy(
            src_ref=part.at[to],
            dst_ref=parts_in.at[NC - 1 - k],
            send_sem=r_sem.at[0],
            recv_sem=r_sem.at[1],
            device_id=(row, to),
            device_id_type=MESH,
        ).start()

    seven(w_iny, w_sem.at[3])
    mid = total(w_iny)
    w_mz[...] = mid
    for peer in z_peers:
        send(w_mz, w_inz.at[z], 2, peer)
    w_inz[z] = mid

    seven(w_inz, w_sem.at[5])
    w_fin[q] = total(w_inz) * scale
    for i, c in q_peers:
        send(w_fin.at[q], w_fin.at[q], 3, (row, over(i, 0, c)))
    whole = parts_in.at[pl.ds(0, NC - 1)]
    pltpu.make_async_copy(whole, whole, r_sem.at[1]).wait()
    mine = acc[pl.ds(pl.multiple_of(col * BLK, BLK), BLK), :]
    for k in range(NC - 1):
        mine = mine + parts_in[k].astype(jnp.float32)
    agg_out[...] = mine.astype(jnp.bfloat16)

    seven(w_fin, w_sem.at[7])
    wg_out[...] = w_fin[...].reshape(BLK, BLK).T

    most = x_v.at[pl.ds(0, NR - 1)]
    pltpu.make_async_copy(most, most, x_send).wait()
    pltpu.make_async_copy(all_g, all_g, g_sem.at[0]).wait()
    sibling.wait_send()
    pltpu.make_async_copy(whole, whole, r_sem.at[0]).wait()
    for k, buf in enumerate((w_in1, w_iny, w_inz, w_fin)):
        seven(buf, w_sem.at[2 * k])


def finish(agg, wg, grad, agg_out, wg_out, grad_out):
    agg_out[...] = agg[...]
    wg_out[...] = wg[...]
    grad_out[...] = grad[...]


def per_device(
    features, adj_blocks, block_rows, block_cols, block_counts, weight, pre_act, upstream
):
    blocks = adj_blocks[0, 0]
    slots = blocks.shape[0]
    vmem = pl.BlockSpec(memory_space=pltpu.VMEM)
    hbm = pl.BlockSpec(memory_space=pltpu.HBM)
    bf16, f32 = jnp.bfloat16, jnp.float32
    nodes = BLK * NR * NC
    wide = (8, SLICE, BLK)
    dma = pltpu.SemaphoreType.DMA
    results = pl.pallas_call(
        functools.partial(kernel, 1.0 / math.sqrt(nodes)),
        out_shape=(
            jax.ShapeDtypeStruct((BLK, BLK), bf16),
            jax.ShapeDtypeStruct((BLK, BLK), f32),
            jax.ShapeDtypeStruct((BLK, BLK), bf16),
        ),
        in_specs=[hbm] * 8,
        out_specs=(vmem, vmem, vmem),
        scratch_shapes=[
            pltpu.SMEM((NR * NC // BLK, BLK), jnp.int32),
            pltpu.VMEM((NR * NC // BLK, BLK), jnp.int32),
            pltpu.VMEM((1, slots), jnp.int32),
            pltpu.VMEM((1, slots), jnp.int32),
            pltpu.SMEM((1, 1), jnp.int32),
            pltpu.VMEM((BLK, BLK), bf16),
            pltpu.VMEM((BLK, BLK), bf16),
            pltpu.VMEM((BLK, BLK), bf16),
            pltpu.VMEM((slots + 1, BLK, BLK), bf16),
            pltpu.VMEM((NR, BLK, BLK), bf16),
            pltpu.VMEM((2, NQ, BLK, BLK), bf16),
            pltpu.VMEM((NR, BLK, BLK), bf16),
            pltpu.VMEM((ROWS, BLK), f32),
            pltpu.VMEM((NC, BLK, BLK), bf16),
            pltpu.VMEM((NC, BLK, BLK), bf16),
            pltpu.VMEM(wide, f32),
            pltpu.VMEM(wide, f32),
            pltpu.VMEM((SLICE, BLK), f32),
            pltpu.VMEM(wide, f32),
            pltpu.VMEM((SLICE, BLK), f32),
            pltpu.VMEM(wide, f32),
            pltpu.VMEM(wide, f32),
            dma((8,)),
            dma,
            dma((NR,)),
            dma((4,)),
            dma((2,)),
            dma((8,)),
        ],
        compiler_params=pltpu.CompilerParams(
            collective_id=0, has_side_effects=True, vmem_limit_bytes=VMEM_BYTES
        ),
        name="gcn",
    )(
        block_rows[0],
        block_cols[0],
        block_counts,
        features,
        blocks,
        weight,
        pre_act,
        upstream,
    )
    return pl.pallas_call(
        finish,
        out_shape=tuple(jax.ShapeDtypeStruct(r.shape, r.dtype) for r in results),
        in_specs=[vmem] * 3,
        out_specs=(vmem, vmem, vmem),
        compiler_params=pltpu.CompilerParams(vmem_limit_bytes=VMEM_BYTES),
        name="finish",
    )(*results)


def solution(mesh):
    placed = (
        P(("col", "row"), None),
        P("row", "col", None, None, None),
        P("row", "col", None),
        P("row", "col", None),
        P("row", "col"),
        P(),
        P(("row", "col"), None),
        P(("row", "col"), None),
    )
    return jax.shard_map(
        per_device,
        mesh=mesh,
        in_specs=placed,
        out_specs=(P(("row", "col"), None), P(), P(("row", "col"), None)),
        check_vma=False,
    )
```
